32 devices in a mesh: tp: 2 (over core), ep: 16 (over z, y, x).
Axes of the slice: x: 2, y: 2, z: 4, core: 2. Of those that a mesh axis runs over, the one named last changes fastest.
Arguments:
- context: bfloat16 [16, 256, 2048], P('ep', None, 'tp'), may hold values from -6 to 6
- out_weight: bfloat16 [2048, 2048], P('tp'), may hold values from -0.125 to 0.125
- residual_in: bfloat16 [16, 256, 2048], P('ep', 'tp'), may hold values from -6 to 6
- norm_gain: float32 [2048], replicated, may hold values from 0.5 to 1.5
- expert_ids: int32 [16, 256, 2], P('ep', 'tp'), may hold values from 0 to 15, all different within a row; in each aligned block of 128 rows (0 to 127, 128 to 255, ..., all dimensions but the last counted through in order) at most 24 rows name the same one
- gate_weights: float32 [16, 256, 2], P('ep', 'tp'), may hold values from 0.2 to 1
- keep_mask: int32 [16, 256, 2], P('ep', 'tp'), may hold values 0 or 1
- expert_in: bfloat16 [16, 2048, 4096], P('ep', None, 'tp'), may hold values from -0.125 to 0.125
- expert_out: bfloat16 [16, 4096, 2048], P('ep', 'tp'), may hold values from -0.09375 to 0.09375
Outputs:
- layer_out: bfloat16 [16, 256, 2048], P('ep', 'tp')
The draws below stay inside these ranges and needn't reach their ends.
Inputs may be any that keep to these rules, and one draw needn't show every extreme that they name: `expert_ids`: among the 128 tokens of one device (aligned blocks of token rows), at most 24 name any one expert; a token's two experts differ; every expert is named somewhere.
All inputs are finite; a program needn't handle non-finite values. No bound on the sum of `keep_mask` on one device may be relied on, other than what follows from the above.
Results may differ from the reference program's by a relative error of at most 0.0054.
Values may be sent and summed in bfloat16 or wider, within the bound.
A program may use at most 128 MiB of HBM per device.

```python
import math
import jax
import jax.numpy as jnp
import numpy as np
from jax import lax

D = 2048
FF = 4096
TOK_DEV = 128
TOK_EP = 256
EXPERTS = 16
SLOT = 24
N_EP = 16


def set_ends(result, own_key, low, top_value):
    index_at = [jax.random.randint(jax.random.fold_in(own_key, axis), (), 0, length) for axis, length in enumerate(result.shape)]
    main_axis = result.shape.index(max(result.shape))
    next_to = index_at[:main_axis] + [(index_at[main_axis] + 1) % result.shape[main_axis]] + index_at[main_axis + 1:]
    return result.at[tuple(index_at)].set(low).at[tuple(next_to)].set(top_value)


def level_of(key, dims, pieces, low, high):
    def one(position, shards_of):
        draws = jax.random.uniform(jax.random.fold_in(jax.random.fold_in(key, 6), position), (shards_of,), jnp.float32, low / len(pieces), high / len(pieces))
        return jnp.repeat(jnp.exp(draws), dims[position] // shards_of).reshape((-1,) + (1,) * (len(dims) - position - 1))

    factor_of = one(*pieces[0])
    for cut in pieces[1:]:
        factor_of = factor_of * one(*cut)
    return factor_of


def deal_out(own_key, own, number, rows, amount, top, reach, slope):
    ranking = jax.random.permutation(own_key, amount)
    crowded, usual = portions_of(amount, rows * top, reach, slope, True), portions_of(amount, rows * top, reach, slope, False)
    places = jnp.arange(amount)

    def named(sizes, offset_by):
        used = int((sizes > 0).sum())
        fixed = max(1, used // 4)
        passed = fixed + (places - fixed + offset_by * (used - fixed)) % max(1, amount - fixed)
        return jnp.zeros((amount,), jnp.int32).at[ranking[jnp.where(places < fixed, places, passed)]].set(jnp.asarray(sizes, jnp.int32))

    sizes = jnp.where(number % 4 == 0, named(crowded, number // 4), named(usual, number - number // 4 - 1))
    mixed = jax.random.permutation(jax.random.fold_in(own, 3), amount)
    donor, receiver = mixed[0:amount // 2 * 2:2], mixed[1:amount // 2 * 2:2]
    margin = jnp.minimum(sizes[donor] - 1, reach - sizes[receiver]) // 2
    margin = jnp.where((donor == ranking[0]) | (receiver == ranking[0]) | (sizes[receiver] == 0), 0, jnp.maximum(margin, 0))
    passed = jax.random.randint(jax.random.fold_in(own, 4), (amount // 2,), 0, 1 << 20) % (margin + 1)
    sizes = sizes.at[donor].add(-passed).at[receiver].add(passed)
    members = jnp.searchsorted(jnp.cumsum(sizes), jnp.arange(rows * top), side="right").astype(jnp.int32)
    listing = members.reshape(top, rows).T
    listing = listing[jax.random.permutation(jax.random.fold_in(own, 1), rows)]
    offset_by = jax.random.randint(jax.random.fold_in(own, 2), (rows, 1), 0, top)
    return jnp.take_along_axis(listing, (jnp.arange(top)[None, :] + offset_by) % top, axis=1)


def portions_of(amount, total, most, skew, full):
    loads = [(1 << 20) // math.isqrt(standing ** skew) + 1 for standing in range(1, amount + 1)]
    largest = most if full else min(most, max(-(-total // amount), total * loads[0] // sum(loads)))
    least = 1 if total - largest >= amount - 1 else 0
    holding, surplus = [largest] + [least] * (amount - 1), total - largest - least * (amount - 1)
    while surplus > 0:
        free = [i for i in range(1, amount) if holding[i] < largest] or [i for i in range(1, amount) if holding[i] < most]
        pool, remaining = sum([loads[i] for i in free]), surplus
        for i in free:
            more = min(most - holding[i], max(1, remaining * loads[i] // pool), surplus)
            holding[i] = holding[i] + more
            surplus = surplus - more
    return np.array(holding)


def noise(rng, dims, width, limit, pieces=(), kind=jnp.bfloat16):
    array = jax.random.normal(rng, dims, jnp.float32) * width
    if len(pieces) > 0:
        array = level_of(rng, dims, pieces, -0.22, 0.18) * array
    return jnp.clip(array, min=-limit, max=limit).astype(kind)


def setup_inputs(seed: int = 0) -> dict:
    seeds = jax.random.split(jax.random.key(seed), 10)
    context = noise(seeds[0], (N_EP, TOK_EP, D), 1.0, 6.0, ((0, 16), (2, 2)))
    out_weight = noise(seeds[1], (D, D), D ** -0.5, 0.125, ((0, 2),))
    residual_in = noise(seeds[2], (N_EP, TOK_EP, D), 1.0, 6.0, ((0, 16), (1, 2)))
    norm_gain = jnp.clip(1.0 + 0.1 * jax.random.normal(seeds[3], (D,), jnp.float32), 0.5, 1.5)
    expert_ids_keys = jax.random.split(jax.random.fold_in(seeds[4], 1), N_EP * TOK_EP // TOK_DEV)
    expert_ids_turns = jax.random.permutation(jax.random.fold_in(seeds[4], 3), N_EP * TOK_EP // TOK_DEV)
    expert_ids = jax.vmap(lambda own, number: deal_out(jax.random.fold_in(seeds[4], 2), own, number, TOK_DEV, EXPERTS, 2, SLOT, 2))(expert_ids_keys, expert_ids_turns).reshape((N_EP, TOK_EP, 2))
    gate_weights = jnp.clip(0.2 + 0.8 * jax.random.uniform(seeds[5], (N_EP, TOK_EP, 2), jnp.float32) ** level_of(seeds[5], (N_EP, TOK_EP, 2), ((0, 16), (1, 2)), -0.2, 0.2), 0.2, 1.0)
    keep_mask = set_ends((jax.random.randint(seeds[6], (N_EP, TOK_EP, 2), 0, 8) < 7).astype(jnp.int32), jax.random.fold_in(seeds[6], 1), 0, 1)
    expert_in = noise(seeds[7], (EXPERTS, D, FF), D ** -0.5, 0.125, ((0, 16), (2, 2)))
    expert_out = noise(seeds[8], (EXPERTS, FF, D), FF ** -0.5, 0.09375, ((0, 16), (1, 2)))
    return dict(context=context, out_weight=out_weight, residual_in=residual_in, norm_gain=norm_gain, expert_ids=expert_ids, gate_weights=gate_weights, keep_mask=keep_mask, expert_in=expert_in, expert_out=expert_out)


def reference(context, out_weight, residual_in, norm_gain, expert_ids, gate_weights, keep_mask, expert_in, expert_out):
    flat_context = context.reshape(-1, D)
    attended = jnp.dot(flat_context, out_weight, preferred_element_type=jnp.float32)
    stream = (residual_in.reshape(-1, D).astype(jnp.float32) + attended).astype(jnp.bfloat16)
    stream_f32 = stream.astype(jnp.float32)
    average = lax.optimization_barrier(jnp.mean(stream_f32, axis=1, keepdims=True))
    centred = stream_f32 - average
    variance = lax.optimization_barrier(jnp.mean(centred * centred, axis=1, keepdims=True))
    normed = (centred / jnp.sqrt(variance + 1e-05) * norm_gain[None, :]).astype(jnp.bfloat16)
    routed = expert_ids.reshape(-1)
    kept_flags = keep_mask.reshape(-1)
    assign_count = routed.shape[0]
    row_bound = 2 * N_EP * SLOT

    def one_expert(collected, inputs):
        expert_index, weight_in, weight_out = inputs
        chosen = (routed == expert_index) & (kept_flags > 0)
        positions = jnp.nonzero(chosen, size=row_bound, fill_value=assign_count)[0].astype(jnp.int32)
        picked_rows = normed[jnp.minimum(positions, assign_count - 1) // 2]
        hidden = jnp.maximum(jnp.dot(picked_rows, weight_in, preferred_element_type=jnp.float32), 0.0).astype(jnp.bfloat16)
        expert_rows = jnp.dot(hidden, weight_out, preferred_element_type=jnp.float32).astype(jnp.bfloat16)
        return (collected.at[positions].set(expert_rows, mode='drop'), None)
    collected, _ = lax.scan(one_expert, jnp.zeros((assign_count, D), jnp.bfloat16), (jnp.arange(EXPERTS, dtype=jnp.int32), expert_in, expert_out))
    gate_flat = jnp.where(kept_flags > 0, gate_weights.reshape(-1), 0.0).astype(jnp.float32)
    mixed = gate_flat[:, None] * collected.astype(jnp.float32)
    mixed = lax.optimization_barrier(jnp.sum(mixed.reshape(-1, 2, D), axis=1))
    layer_out = (stream_f32 + mixed).astype(jnp.bfloat16)
    return layer_out.reshape(N_EP, TOK_EP, D)
```

```python
import functools

import jax
import jax.numpy as jnp
from jax import lax
from jax.experimental import pallas as pl
from jax.experimental.pallas import tpu as pltpu
from jax.sharding import PartitionSpec as P

GROUP = 4
F32 = jnp.float32
BF16 = jnp.bfloat16
MESH = pl.DeviceIdType.MESH


def far_first(step, count):
    odd = step % 2
    return count // 2 + (step // 2) * (1 - odd) - ((step + 1) // 2) * odd


def near_then_far(step, count):
    later = jnp.minimum(step, 1)
    return far_first(jnp.maximum(step - 1, 0), count) * later


def kernel(
    n, cap, cap2,
    ctx, res, gain, raw, wo, w1, w2,
    out,
    wo_v, w1_v, w2_v,
    psend, precv, pown, stream_v, nfull, nrm, meta,
    xsend, xrecv, h_v, yo, ps, pr, ysend, yrecv, mixed, mrecv,
    wsem, pair_send, pair_recv,
    xs_send, xs_recv, fw_send, fw_recv, pt_send, pt_recv, ys_send, ys_recv, self_sem,
):
    tok, width = res.shape
    half = width // 2
    ff = w1.shape[1]
    groups = n // GROUP
    rows = GROUP * cap2
    c = lax.axis_index("tp")
    me = lax.axis_index("ep")
    o = 1 - c
    plane = me // GROUP

    def remote(src, dst, send, recv, **target):
        return pltpu.make_async_remote_copy(
            src_ref=src, dst_ref=dst, send_sem=send, recv_sem=recv,
            device_id=target, device_id_type=MESH,
        )

    load_wo = pltpu.make_async_copy(wo, wo_v, wsem.at[0])
    load_w1 = pltpu.make_async_copy(w1, w1_v, wsem.at[1])
    load_w2 = pltpu.make_async_copy(w2, w2_v, wsem.at[2])
    load_wo.start()
    load_w1.start()
    load_w2.start()

    barrier = pltpu.get_barrier_semaphore()
    pl.semaphore_signal(barrier, inc=1, device_id={"tp": o}, device_id_type=MESH)

    @pl.loop(0, n - 1)
    def _(i):
        pl.semaphore_signal(
            barrier, inc=1, device_id={"ep": (me + 1 + i) % n}, device_id_type=MESH
        )

    experts = lax.broadcasted_iota(jnp.int32, (n, tok), 0).astype(F32)
    before = (
        lax.broadcasted_iota(jnp.int32, (tok, tok), 0)
        < lax.broadcasted_iota(jnp.int32, (tok, tok), 1)
    ).astype(F32).astype(BF16)
    table = raw[...]
    ahead = jnp.zeros((n, 1), F32)
    slots, gates = [], []
    for k in range(2):
        keep = table[2 + k:3 + k]
        hot = jnp.where(experts == table[k:k + 1], keep, 0.0)
        rank = jnp.dot(hot.astype(BF16), before, preferred_element_type=F32) + ahead
        place = jnp.sum(hot * (rank + experts * cap2), axis=0, keepdims=True)
        slots.append(jnp.where(keep > 0, place + (c * cap).astype(F32), -1.0))
        gates.append(jnp.where(keep > 0, table[4 + k:5 + k], 0.0))
        ahead = jnp.sum(hot, axis=1, keepdims=True)
    meta[c] = jnp.concatenate(slots + gates + [jnp.zeros((4, tok), F32)], axis=0)

    load_wo.wait()
    tile = 512

    @pl.loop(0, width // tile)
    def _(t):
        cols = pl.ds(pl.multiple_of(t * tile, tile), tile)
        psend[:, cols] = jnp.dot(
            ctx[pl.ds(o * tok, tok), :], wo_v[:, cols], preferred_element_type=F32
        )

    pl.semaphore_wait(barrier, n)
    send_p = remote(psend, precv, pair_send.at[0], pair_recv.at[0], tp=o)
    send_p.start()
    send_meta = remote(meta.at[c], meta.at[c], pair_send.at[1], pair_recv.at[1], tp=o)
    send_meta.start()

    @pl.loop(0, width // tile)
    def _(t):
        cols = pl.ds(pl.multiple_of(t * tile, tile), tile)
        pown[:, cols] = jnp.dot(
            ctx[pl.ds(c * tok, tok), :], wo_v[:, cols], preferred_element_type=F32
        )

    send_p.wait_recv()

    @pl.loop(0, tok // 16)
    def _(i):
        r = pl.ds(pl.multiple_of(i * 16, 16), 16)
        stream = (res[r, :].astype(F32) + (pown[r, :] + precv[r, :])).astype(BF16)
        stream_v[r, :] = stream
        stream = stream.astype(F32)
        centred = stream - jnp.mean(stream, axis=1, keepdims=True)
        variance = jnp.mean(centred * centred, axis=1, keepdims=True)
        normed = (centred / jnp.sqrt(variance + 1e-05) * gain[...]).astype(BF16)
        nfull[0, r, :] = normed[:, :half]
        nfull[1, r, :] = normed[:, half:]

    send_n = remote(nfull.at[o], nrm.at[c], pair_send.at[2], pair_recv.at[2], tp=o)
    send_n.start()
    nrm[c] = nfull[c]
    remote(meta.at[c], meta.at[o], pair_send.at[1], pair_recv.at[1], tp=o).wait_recv()
    remote(nfull.at[o], nrm.at[o], pair_send.at[2], pair_recv.at[2], tp=o).wait_recv()

    def lanes(row):
        return jnp.concatenate([meta[0, row:row + 1, :], meta[1, row:row + 1, :]], axis=1)

    def matches(q):
        index = (lax.broadcasted_iota(jnp.int32, (rows, 2 * tok), 0) + q * rows).astype(F32)
        return index == lanes(0), index == lanes(1)

    @pl.loop(0, groups)
    def _(step):
        q = (plane + far_first(step, groups)) % groups
        first, second = matches(q)
        pick = jnp.where(first | second, 1.0, 0.0).astype(BF16)
        picked = jnp.dot(
            pick, nrm[...].reshape(2 * tok, half), preferred_element_type=F32
        ).astype(BF16)
        xsend[pl.ds(q * GROUP, GROUP)] = picked.reshape(GROUP, cap2, half)
        for j in range(GROUP):
            e = q * GROUP + j

            @pl.when(e != me)
            def _():
                remote(
                    xsend.at[e], xrecv.at[c, me], xs_send.at[e], xs_recv.at[me], ep=e
                ).start()

            @pl.when(e == me)
            def _():
                pltpu.make_async_copy(xsend.at[e], xrecv.at[c, me], self_sem.at[0]).start()

    load_w1.wait()
    load_w2.wait()

    @pl.loop(0, groups)
    def _(step):
        q = (plane + groups - near_then_far(step, groups)) % groups
        block = pl.ds(q * GROUP, GROUP)
        for j in range(GROUP):
            e = q * GROUP + j

            @pl.when(e != me)
            def _():
                remote(
                    xsend.at[e], xrecv.at[c, e], xs_send.at[e], xs_recv.at[e], ep=e
                ).wait_recv()

            @pl.when(e == me)
            def _():
                pltpu.make_async_copy(xsend.at[e], xrecv.at[c, me], self_sem.at[0]).wait()

        remote(
            xrecv.at[c, block], xrecv.at[c, block], fw_send.at[q], fw_recv.at[q], tp=o
        ).start()
        remote(
            xrecv.at[c, block], xrecv.at[o, block], fw_send.at[q], fw_recv.at[q], tp=o
        ).wait_recv()

        @pl.loop(0, ff // tile)
        def _(t):
            cols = pl.ds(pl.multiple_of(t * tile, tile), tile)
            hidden = jnp.dot(
                xrecv[0, block].reshape(rows, half), w1_v[:half, cols],
                preferred_element_type=F32,
            ) + jnp.dot(
                xrecv[1, block].reshape(rows, half), w1_v[half:, cols],
                preferred_element_type=F32,
            )
            h_v[:, cols] = jnp.maximum(hidden, 0.0).astype(BF16)

        @pl.loop(0, half // tile)
        def _(t):
            cols = pl.ds(pl.multiple_of(t * tile, tile), tile)
            ps[q, :, cols] = jnp.dot(
                h_v[...], w2_v[:, pl.ds(pl.multiple_of(o * half + t * tile, tile), tile)],
                preferred_element_type=F32,
            )

        part = remote(ps.at[q], pr.at[q], pt_send.at[q], pt_recv.at[q], tp=o)
        part.start()

        @pl.loop(0, half // tile)
        def _(t):
            cols = pl.ds(pl.multiple_of(t * tile, tile), tile)
            yo[:, cols] = jnp.dot(
                h_v[...], w2_v[:, pl.ds(pl.multiple_of(c * half + t * tile, tile), tile)],
                preferred_element_type=F32,
            )

        part.wait_recv()
        ysend[block] = (yo[...] + pr[q]).astype(BF16).reshape(GROUP, cap2, half)
        for j in range(GROUP):
            e = q * GROUP + j

            @pl.when(e != me)
            def _():
                remote(
                    ysend.at[e], yrecv.at[me], ys_send.at[e], ys_recv.at[me], ep=e
                ).start()

            @pl.when(e == me)
            def _():
                pltpu.make_async_copy(ysend.at[e], yrecv.at[me], self_sem.at[1]).start()

    mixed[...] = jnp.zeros_like(mixed)

    @pl.loop(0, groups)
    def _(step):
        q = (plane + near_then_far(step, groups)) % groups
        for j in range(GROUP):
            e = q * GROUP + j

            @pl.when(e != me)
            def _():
                remote(
                    ysend.at[e], yrecv.at[e], ys_send.at[e], ys_recv.at[e], ep=e
                ).wait_recv()

            @pl.when(e == me)
            def _():
                pltpu.make_async_copy(ysend.at[e], yrecv.at[me], self_sem.at[1]).wait()

        first, second = matches(q)
        weight = jnp.where(first, lanes(2), 0.0) + jnp.where(second, lanes(3), 0.0)
        high = weight.astype(BF16)
        low = (weight - high.astype(F32)).astype(BF16)
        values = yrecv[pl.ds(q * GROUP, GROUP)].reshape(rows, half)
        dims = (((0,), (0,)), ((), ()))
        added = lax.dot_general(high, values, dims, preferred_element_type=F32)
        added += lax.dot_general(low, values, dims, preferred_element_type=F32)
        mixed[...] += added.reshape(2, tok, half)

    send_m = remote(mixed.at[o], mrecv, pair_send.at[3], pair_recv.at[3], tp=o)
    send_m.start()
    own = pl.ds(pl.multiple_of(c * half, half), half)
    other = pl.ds(pl.multiple_of(o * half, half), half)
    out[:, own] = (stream_v[:, own].astype(F32) + mixed[c]).astype(BF16)
    send_m.wait_recv()
    out[:, other] = (stream_v[:, other].astype(F32) + mrecv[...]).astype(BF16)

    send_p.wait_send()
    send_meta.wait_send()
    send_n.wait_send()
    send_m.wait_send()

    @pl.loop(0, n - 1)
    def _(i):
        e = (me + 1 + i) % n
        remote(xsend.at[e], xrecv.at[c, me], xs_send.at[e], xs_recv.at[me], ep=e).wait_send()
        remote(ysend.at[e], yrecv.at[me], ys_send.at[e], ys_recv.at[me], ep=e).wait_send()

    @pl.loop(0, groups)
    def _(q):
        block = pl.ds(q * GROUP, GROUP)
        remote(
            xrecv.at[c, block], xrecv.at[c, block], fw_send.at[q], fw_recv.at[q], tp=o
        ).wait_send()
        remote(ps.at[q], pr.at[q], pt_send.at[q], pt_recv.at[q], tp=o).wait_send()


def body(
    n,
    context,
    out_weight,
    residual_in,
    norm_gain,
    expert_ids,
    gate_weights,
    keep_mask,
    expert_in,
    expert_out,
):
    tok, width = residual_in.shape[1:]
    heads = out_weight.shape[0]
    ff = expert_in.shape[2]
    half = width // 2
    cap = 3 * tok // n
    cap2 = -(-2 * cap // 16) * 16
    groups = n // GROUP
    rows = GROUP * cap2
    raw = jnp.concatenate(
        [
            expert_ids[0].astype(F32),
            keep_mask[0].astype(F32),
            gate_weights[0],
            jnp.zeros((tok, 2), F32),
        ],
        axis=1,
    ).T
    vmem = pl.BlockSpec(memory_space=pltpu.VMEM)
    hbm = pl.BlockSpec(memory_space=pl.ANY)
    dma = pltpu.SemaphoreType.DMA
    result = pl.pallas_call(
        functools.partial(kernel, n, cap, cap2),
        out_shape=jax.ShapeDtypeStruct((tok, width), BF16),
        in_specs=[vmem, vmem, vmem, vmem, hbm, hbm, hbm],
        out_specs=vmem,
        scratch_shapes=[
            pltpu.VMEM((heads, width), BF16),
            pltpu.VMEM((width, ff), BF16),
            pltpu.VMEM((ff, width), BF16),
            pltpu.VMEM((tok, width), F32),
            pltpu.VMEM((tok, width), F32),
            pltpu.VMEM((tok, width), F32),
            pltpu.VMEM((tok, width), BF16),
            pltpu.VMEM((2, tok, half), BF16),
            pltpu.VMEM((2, tok, half), BF16),
            pltpu.VMEM((2, 8, tok), F32),
            pltpu.VMEM((n, cap2, half), BF16),
            pltpu.VMEM((2, n, cap2, half), BF16),
            pltpu.VMEM((rows, ff), BF16),
            pltpu.VMEM((rows, half), F32),
            pltpu.VMEM((groups, rows, half), F32),
            pltpu.VMEM((groups, rows, half), F32),
            pltpu.VMEM((n, cap2, half), BF16),
            pltpu.VMEM((n, cap2, half), BF16),
            pltpu.VMEM((2, tok, half), F32),
            pltpu.VMEM((tok, half), F32),
            dma((3,)), dma((4,)), dma((4,)),
            dma((n,)), dma((n,)), dma((groups,)), dma((groups,)),
            dma((groups,)), dma((groups,)), dma((n,)), dma((n,)), dma((2,)),
        ],
        compiler_params=pltpu.CompilerParams(
            collective_id=0, has_side_effects=True, vmem_limit_bytes=60 * 2**20
        ),
    )(context[0], residual_in[0], norm_gain[None, :], raw, out_weight, expert_in[0], expert_out[0])
    return result[None]


def solution(mesh):
    return jax.shard_map(
        functools.partial(body, mesh.shape["ep"]),
        mesh=mesh,
        in_specs=(
            P("ep", None, "tp"),
            P("tp", None),
            P("ep", "tp", None),
            P(),
            P("ep", "tp", None),
            P("ep", "tp", None),
            P("ep", "tp", None),
            P("ep", None, "tp"),
            P("ep", "tp", None),
        ),
        out_specs=P("ep", "tp", None),
        check_vma=False,
    )
```

```python
import functools

import jax
import jax.numpy as jnp
from jax import lax
from jax.experimental import pallas as pl
from jax.experimental.pallas import tpu as pltpu
from jax.sharding import PartitionSpec as P

GROUP = 4
F32 = jnp.float32
BF16 = jnp.bfloat16
MESH = pl.DeviceIdType.MESH


def far_first(step, count):
    odd = step % 2
    return count // 2 + (step // 2) * (1 - odd) - ((step + 1) // 2) * odd


def near_then_far(step, count):
    later = jnp.minimum(step, 1)
    return far_first(jnp.maximum(step - 1, 0), count) * later


def kernel(
    n, cap, cap2,
    ctx, res, gain, ids, gate, kept, wo, w1, w2,
    out,
    wo_v, w1_v, w2_v,
    both, precv, stream_v, nfull, nrm, meta,
    xsend, xrecv, h_v, yo, ps, pr, ysend, yrecv, mixed, mrecv,
    wsem, pair_send, pair_recv,
    xs_send, xs_recv, fw_send, fw_recv, pt_send, pt_recv, ys_send, ys_recv, self_sem,
):
    tok, width = res.shape
    half = width // 2
    ff = w1.shape[1]
    groups = n // GROUP
    rows = GROUP * cap2
    c = lax.axis_index("tp")
    me = lax.axis_index("ep")
    o = 1 - c
    plane = me // GROUP

    def remote(src, dst, send, recv, **target):
        return pltpu.make_async_remote_copy(
            src_ref=src, dst_ref=dst, send_sem=send, recv_sem=recv,
            device_id=target, device_id_type=MESH,
        )

    tile = 512
    tiles = width // tile
    load_wo = [
        pltpu.make_async_copy(
            wo.at[:, t * tile:(t + 1) * tile], wo_v.at[:, t * tile:(t + 1) * tile], wsem.at[2 + t]
        )
        for t in range(tiles)
    ]
    load_w1 = pltpu.make_async_copy(w1, w1_v, wsem.at[0])
    load_w2 = pltpu.make_async_copy(w2, w2_v, wsem.at[1])
    for load in load_wo:
        load.start()

    barrier = pltpu.get_barrier_semaphore()
    pl.semaphore_signal(barrier, inc=1, device_id={"tp": o}, device_id_type=MESH)

    @pl.loop(0, n - 1)
    def _(i):
        pl.semaphore_signal(
            barrier, inc=1, device_id={"ep": (me + 1 + i) % n}, device_id_type=MESH
        )

    experts = lax.broadcasted_iota(jnp.int32, (n, tok), 0).astype(F32)
    before = (
        lax.broadcasted_iota(jnp.int32, (tok, tok), 0)
        < lax.broadcasted_iota(jnp.int32, (tok, tok), 1)
    ).astype(F32).astype(BF16)
    ahead = jnp.zeros((n, 1), F32)
    slots, gates = [], []
    for k in range(2):
        keep = kept[k:k + 1].astype(F32)
        hot = jnp.where(experts == ids[k:k + 1].astype(F32), keep, 0.0)
        rank = jnp.dot(hot.astype(BF16), before, preferred_element_type=F32) + ahead
        place = jnp.sum(hot * (rank + experts * cap2), axis=0, keepdims=True)
        slots.append(jnp.where(keep > 0, place + (c * cap).astype(F32), -1.0))
        gates.append(jnp.where(keep > 0, gate[k:k + 1], 0.0))
        ahead = jnp.sum(hot, axis=1, keepdims=True)
    meta[c] = jnp.concatenate(slots + gates + [jnp.zeros((4, tok), F32)], axis=0)

    send_p = []
    for t in range(tiles):
        cols = pl.ds(t * tile, tile)
        load_wo[t].wait()
        if t == tiles - 1:
            load_w1.start()
            load_w2.start()
        both[:, :, cols] = jnp.dot(
            ctx[...], wo_v[:, cols], preferred_element_type=F32
        ).reshape(2, tok, tile)
        if t == 0:
            pl.semaphore_wait(barrier, n)
        send_p.append(remote(
            both.at[o, :, cols], precv.at[:, cols],
            pair_send.at[4 + t], pair_recv.at[4 + t], tp=o,
        ))
        send_p[t].start()
    send_meta = remote(meta.at[c], meta.at[c], pair_send.at[1], pair_recv.at[1], tp=o)
    send_meta.start()
    for send in send_p:
        send.wait_recv()

    send_n = []
    for part in range(2):
        top = part * (tok // 2)

        @pl.loop(0, tok // 32, unroll=2)
        def _(i):
            r = pl.ds(pl.multiple_of(top + i * 16, 16), 16)
            stream = (res[r, :].astype(F32) + (both[c, r, :] + precv[r, :])).astype(BF16)
            stream_v[r, :] = stream
            stream = stream.astype(F32)
            centred = stream - jnp.mean(stream, axis=1, keepdims=True)
            variance = jnp.mean(centred * centred, axis=1, keepdims=True)
            normed = (centred * (1.0 / jnp.sqrt(variance + 1e-05)) * gain[...]).astype(BF16)
            nfull[0, r, :] = normed[:, :half]
            nfull[1, r, :] = normed[:, half:]

        r = pl.ds(top, tok // 2)
        sem = 2 * part
        send_n.append(remote(
            nfull.at[o, r], nrm.at[c, r], pair_send.at[sem], pair_recv.at[sem], tp=o
        ))
        send_n[part].start()
        nrm[c, r] = nfull[c, r]

    remote(meta.at[c], meta.at[o], pair_send.at[1], pair_recv.at[1], tp=o).wait_recv()
    for part in range(2):
        r = pl.ds(part * (tok // 2), tok // 2)
        sem = 2 * part
        remote(
            nfull.at[o, r], nrm.at[o, r], pair_send.at[sem], pair_recv.at[sem], tp=o
        ).wait_recv()

    def lanes(row):
        return jnp.concatenate([meta[0, row:row + 1, :], meta[1, row:row + 1, :]], axis=1)

    def matches(q):
        index = (lax.broadcasted_iota(jnp.int32, (rows, 2 * tok), 0) + q * rows).astype(F32)
        return index == lanes(0), index == lanes(1)

    @pl.loop(0, groups)
    def _(step):
        q = (plane + far_first(step, groups)) % groups
        first, second = matches(q)
        pick = jnp.where(first | second, 1.0, 0.0).astype(BF16)
        picked = jnp.dot(
            pick, nrm[...].reshape(2 * tok, half), preferred_element_type=F32
        ).astype(BF16)
        xsend[pl.ds(q * GROUP, GROUP)] = picked.reshape(GROUP, cap2, half)
        for j in range(GROUP):
            e = q * GROUP + j

            @pl.when(e != me)
            def _():
                remote(
                    xsend.at[e], xrecv.at[c, me], xs_send.at[e], xs_recv.at[me], ep=e
                ).start()

            @pl.when(e == me)
            def _():
                pltpu.make_async_copy(xsend.at[e], xrecv.at[c, me], self_sem.at[0]).start()

    load_w1.wait()
    load_w2.wait()

    @pl.loop(0, groups)
    def _(step):
        q = (plane + groups - near_then_far(step, groups)) % groups
        block = pl.ds(q * GROUP, GROUP)
        for j in range(GROUP):
            e = q * GROUP + j

            @pl.when(e != me)
            def _():
                remote(
                    xsend.at[e], xrecv.at[c, e], xs_send.at[e], xs_recv.at[e], ep=e
                ).wait_recv()

            @pl.when(e == me)
            def _():
                pltpu.make_async_copy(xsend.at[e], xrecv.at[c, me], self_sem.at[0]).wait()

        remote(
            xrecv.at[c, block], xrecv.at[c, block], fw_send.at[q], fw_recv.at[q], tp=o
        ).start()
        remote(
            xrecv.at[c, block], xrecv.at[o, block], fw_send.at[q], fw_recv.at[q], tp=o
        ).wait_recv()

        @pl.loop(0, ff // tile)
        def _(t):
            cols = pl.ds(pl.multiple_of(t * tile, tile), tile)
            hidden = jnp.dot(
                xrecv[0, block].reshape(rows, half), w1_v[:half, cols],
                preferred_element_type=F32,
            ) + jnp.dot(
                xrecv[1, block].reshape(rows, half), w1_v[half:, cols],
                preferred_element_type=F32,
            )
            h_v[:, cols] = jnp.maximum(hidden, 0.0).astype(BF16)

        @pl.loop(0, half // tile)
        def _(t):
            cols = pl.ds(pl.multiple_of(t * tile, tile), tile)
            ps[q, :, cols] = jnp.dot(
                h_v[...], w2_v[:, pl.ds(pl.multiple_of(o * half + t * tile, tile), tile)],
                preferred_element_type=F32,
            )

        part = remote(ps.at[q], pr.at[q], pt_send.at[q], pt_recv.at[q], tp=o)
        part.start()

        @pl.loop(0, half // tile)
        def _(t):
            cols = pl.ds(pl.multiple_of(t * tile, tile), tile)
            yo[:, cols] = jnp.dot(
                h_v[...], w2_v[:, pl.ds(pl.multiple_of(c * half + t * tile, tile), tile)],
                preferred_element_type=F32,
            )

        part.wait_recv()
        ysend[block] = (yo[...] + pr[q]).astype(BF16).reshape(GROUP, cap2, half)
        for j in range(GROUP):
            e = q * GROUP + j

            @pl.when(e != me)
            def _():
                remote(
                    ysend.at[e], yrecv.at[me], ys_send.at[e], ys_recv.at[me], ep=e
                ).start()

            @pl.when(e == me)
            def _():
                pltpu.make_async_copy(ysend.at[e], yrecv.at[me], self_sem.at[1]).start()

    mixed[...] = jnp.zeros_like(mixed)

    @pl.loop(0, groups)
    def _(step):
        q = (plane + near_then_far(step, groups)) % groups
        for j in range(GROUP):
            e = q * GROUP + j

            @pl.when(e != me)
            def _():
                remote(
                    ysend.at[e], yrecv.at[e], ys_send.at[e], ys_recv.at[e], ep=e
                ).wait_recv()

            @pl.when(e == me)
            def _():
                pltpu.make_async_copy(ysend.at[e], yrecv.at[me], self_sem.at[1]).wait()

        first, second = matches(q)
        weight = jnp.where(first, lanes(2), 0.0) + jnp.where(second, lanes(3), 0.0)
        high = weight.astype(BF16)
        low = (weight - high.astype(F32)).astype(BF16)
        values = yrecv[pl.ds(q * GROUP, GROUP)].reshape(rows, half)
        dims = (((0,), (0,)), ((), ()))
        added = lax.dot_general(high, values, dims, preferred_element_type=F32)
        added += lax.dot_general(low, values, dims, preferred_element_type=F32)
        mixed[...] += added.reshape(2, tok, half)

    send_m = remote(mixed.at[o], mrecv, pair_send.at[3], pair_recv.at[3], tp=o)
    send_m.start()
    own = pl.ds(pl.multiple_of(c * half, half), half)
    other = pl.ds(pl.multiple_of(o * half, half), half)
    out[:, own] = (stream_v[:, own].astype(F32) + mixed[c]).astype(BF16)
    send_m.wait_recv()
    out[:, other] = (stream_v[:, other].astype(F32) + mrecv[...]).astype(BF16)

    for send in send_p + send_n:
        send.wait_send()
    send_meta.wait_send()
    send_m.wait_send()

    @pl.loop(0, n - 1)
    def _(i):
        e = (me + 1 + i) % n
        remote(xsend.at[e], xrecv.at[c, me], xs_send.at[e], xs_recv.at[me], ep=e).wait_send()
        remote(ysend.at[e], yrecv.at[me], ys_send.at[e], ys_recv.at[me], ep=e).wait_send()

    @pl.loop(0, groups)
    def _(q):
        block = pl.ds(q * GROUP, GROUP)
        remote(
            xrecv.at[c, block], xrecv.at[c, block], fw_send.at[q], fw_recv.at[q], tp=o
        ).wait_send()
        remote(ps.at[q], pr.at[q], pt_send.at[q], pt_recv.at[q], tp=o).wait_send()


def body(
    n,
    context,
    out_weight,
    residual_in,
    norm_gain,
    expert_ids,
    gate_weights,
    keep_mask,
    expert_in,
    expert_out,
):
    tok, width = residual_in.shape[1:]
    heads = out_weight.shape[0]
    ff = expert_in.shape[2]
    half = width // 2
    cap = 3 * tok // n
    cap2 = -(-2 * cap // 16) * 16
    groups = n // GROUP
    rows = GROUP * cap2
    vmem = pl.BlockSpec(memory_space=pltpu.VMEM)
    hbm = pl.BlockSpec(memory_space=pl.ANY)
    dma = pltpu.SemaphoreType.DMA
    result = pl.pallas_call(
        functools.partial(kernel, n, cap, cap2),
        out_shape=jax.ShapeDtypeStruct((tok, width), BF16),
        in_specs=[vmem] * 6 + [hbm, hbm, hbm],
        out_specs=vmem,
        scratch_shapes=[
            pltpu.VMEM((heads, width), BF16),
            pltpu.VMEM((width, ff), BF16),
            pltpu.VMEM((ff, width), BF16),
            pltpu.VMEM((2, tok, width), F32),
            pltpu.VMEM((tok, width), F32),
            pltpu.VMEM((tok, width), BF16),
            pltpu.VMEM((2, tok, half), BF16),
            pltpu.VMEM((2, tok, half), BF16),
            pltpu.VMEM((2, 8, tok), F32),
            pltpu.VMEM((n, cap2, half), BF16),
            pltpu.VMEM((2, n, cap2, half), BF16),
            pltpu.VMEM((rows, ff), BF16),
            pltpu.VMEM((rows, half), F32),
            pltpu.VMEM((groups, rows, half), F32),
            pltpu.VMEM((groups, rows, half), F32),
            pltpu.VMEM((n, cap2, half), BF16),
            pltpu.VMEM((n, cap2, half), BF16),
            pltpu.VMEM((2, tok, half), F32),
            pltpu.VMEM((tok, half), F32),
            dma((6,)), dma((8,)), dma((8,)),
            dma((n,)), dma((n,)), dma((groups,)), dma((groups,)),
            dma((groups,)), dma((groups,)), dma((n,)), dma((n,)), dma((2,)),
        ],
        compiler_params=pltpu.CompilerParams(
            collective_id=0, has_side_effects=True, vmem_limit_bytes=60 * 2**20
        ),
    )(
        context[0], residual_in[0], norm_gain[None, :],
        expert_ids[0].T, gate_weights[0].T, keep_mask[0].T,
        out_weight, expert_in[0], expert_out[0],
    )
    return result[None]


def solution(mesh):
    return jax.shard_map(
        functools.partial(body, mesh.shape["ep"]),
        mesh=mesh,
        in_specs=(
            P("ep", None, "tp"),
            P("tp", None),
            P("ep", "tp", None),
            P(),
            P("ep", "tp", None),
            P("ep", "tp", None),
            P("ep", "tp", None),
            P("ep", None, "tp"),
            P("ep", "tp", None),
        ),
        out_specs=P("ep", "tp", None),
        check_vma=False,
    )
```

```python
import functools

import jax
import jax.numpy as jnp
from jax import lax
from jax.experimental import pallas as pl
from jax.experimental.pallas import tpu as pltpu
from jax.sharding import PartitionSpec as P

F32 = jnp.float32
BF16 = jnp.bfloat16
MESH = pl.DeviceIdType.MESH


def kernel(
    n, cap, cap2, caps,
    ctx, res, gain, ids, gate, kept, wo, w1, w2,
    out,
    wo_v, w1_v, w2_v,
    both, precv, stream_v, nfull, nrm, meta, pnrm, pmeta,
    xsend, xrecv, fsend, frecv, h_v, yo, ps, pr, fpr,
    ysend, yrecv, fysend, fyrecv, cback, cmix, mixed, mrecv,
    wsem, pair_send, pair_recv, tk_send, tk_recv, fw_send, fw_recv, pt_send, pt_recv,
    xs_send, xs_recv, ys_send, ys_recv, ff_send, ff_recv, fy_send, fy_recv,
    cb_send, cb_recv, self_sem,
):
    tok, width = res.shape
    half = width // 2
    ff = w1.shape[1]
    near = n // 2
    c = lax.axis_index("tp")
    me = lax.axis_index("ep")
    o = 1 - c
    base = me // near * near
    mine = me - base
    partner = (me + near) % n

    def remote(src, dst, send, recv, **target):
        return pltpu.make_async_remote_copy(
            src_ref=src, dst_ref=dst, send_sem=send, recv_sem=recv,
            device_id=target, device_id_type=MESH,
        )

    tile = 512
    tiles = width // tile
    load_wo = [
        pltpu.make_async_copy(
            wo.at[:, t * tile:(t + 1) * tile], wo_v.at[:, t * tile:(t + 1) * tile], wsem.at[2 + t]
        )
        for t in range(tiles)
    ]
    load_w1 = pltpu.make_async_copy(w1, w1_v, wsem.at[0])
    load_w2 = pltpu.make_async_copy(w2, w2_v, wsem.at[1])
    for load in load_wo:
        load.start()

    barrier = pltpu.get_barrier_semaphore()
    pl.semaphore_signal(barrier, inc=1, device_id={"tp": o}, device_id_type=MESH)

    pl.semaphore_signal(barrier, inc=1, device_id={"ep": partner}, device_id_type=MESH)

    @pl.loop(0, near - 1)
    def _(i):
        pl.semaphore_signal(
            barrier, inc=1, device_id={"ep": base + (mine + 1 + i) % near}, device_id_type=MESH
        )

    experts = lax.broadcasted_iota(jnp.int32, (n, tok), 0).astype(F32)
    before = (
        lax.broadcasted_iota(jnp.int32, (tok, tok), 0)
        < lax.broadcasted_iota(jnp.int32, (tok, tok), 1)
    ).astype(F32).astype(BF16)
    ahead = jnp.zeros((n, 1), F32)
    slots, gates, places = [], [], []
    for k in range(2):
        keep = kept[k:k + 1].astype(F32)
        hot = jnp.where(experts == ids[k:k + 1].astype(F32), keep, 0.0)
        rank = jnp.dot(hot.astype(BF16), before, preferred_element_type=F32) + ahead
        place = jnp.sum(hot * (rank + experts * cap2), axis=0, keepdims=True)
        slots.append(jnp.where(keep > 0, place + (c * cap).astype(F32), -1.0))
        gates.append(jnp.where(keep > 0, gate[k:k + 1], 0.0))
        place = jnp.sum(hot * (rank + experts * caps), axis=0, keepdims=True)
        places.append(jnp.where(keep > 0, place, -1.0))
        ahead = jnp.sum(hot, axis=1, keepdims=True)
    meta[c] = jnp.concatenate(slots + gates + places + [jnp.zeros((2, tok), F32)], axis=0)

    send_p = []
    for t in range(tiles):
        cols = pl.ds(t * tile, tile)
        load_wo[t].wait()
        if t == tiles - 1:
            load_w1.start()
            load_w2.start()
        both[:, :, cols] = jnp.dot(
            ctx[...], wo_v[:, cols], preferred_element_type=F32
        ).reshape(2, tok, tile)
        if t == 0:
            pl.semaphore_wait(barrier, near + 1)
        send_p.append(remote(
            both.at[o, :, cols], precv.at[:, cols],
            pair_send.at[4 + t], pair_recv.at[4 + t], tp=o,
        ))
        send_p[t].start()
    send_meta = remote(meta.at[c], meta.at[c], pair_send.at[1], pair_recv.at[1], tp=o)
    send_meta.start()
    for send in send_p:
        send.wait_recv()

    send_n = []
    for part in range(2):
        top = part * (tok // 2)

        @pl.loop(0, tok // 32, unroll=2)
        def _(i):
            r = pl.ds(pl.multiple_of(top + i * 16, 16), 16)
            stream = (res[r, :].astype(F32) + (both[c, r, :] + precv[r, :])).astype(BF16)
            stream_v[r, :] = stream
            stream = stream.astype(F32)
            centred = stream - jnp.mean(stream, axis=1, keepdims=True)
            variance = jnp.mean(centred * centred, axis=1, keepdims=True)
            normed = (centred * (1.0 / jnp.sqrt(variance + 1e-05)) * gain[...]).astype(BF16)
            nfull[0, r, :] = normed[:, :half]
            nfull[1, r, :] = normed[:, half:]

        r = pl.ds(top, tok // 2)
        sem = 2 * part
        send_n.append(remote(
            nfull.at[o, r], nrm.at[c, r], pair_send.at[sem], pair_recv.at[sem], tp=o
        ))
        send_n[part].start()
        nrm[c, r] = nfull[c, r]

    remote(meta.at[c], meta.at[o], pair_send.at[1], pair_recv.at[1], tp=o).wait_recv()
    for part in range(2):
        r = pl.ds(part * (tok // 2), tok // 2)
        sem = 2 * part
        remote(
            nfull.at[o, r], nrm.at[o, r], pair_send.at[sem], pair_recv.at[sem], tp=o
        ).wait_recv()

    def lanes(row):
        return jnp.concatenate([meta[0, row:row + 1, :], meta[1, row:row + 1, :]], axis=1)

    def near_matches():
        shape = (near * cap2, 2 * tok)
        index = (lax.broadcasted_iota(jnp.int32, shape, 0) + base * cap2).astype(F32)
        return index == lanes(0), index == lanes(1)

    def far_matches(s):
        shape = (near * caps, tok)
        index = (lax.broadcasted_iota(jnp.int32, shape, 0) + base * caps).astype(F32)
        return index == pmeta[s, 4:5, :], index == pmeta[s, 5:6, :]

    def picked(matches, tokens, shape):
        pick = jnp.where(matches[0] | matches[1], 1.0, 0.0).astype(BF16)
        return jnp.dot(pick, tokens, preferred_element_type=F32).astype(BF16).reshape(shape)

    def spread(src, dst, send, recv, first, own):
        @pl.loop(0, near)
        def _(j):
            @pl.when(j != mine)
            def _():
                remote(
                    src.at[j], dst.at[mine], send.at[first + j], recv.at[first + mine],
                    ep=base + j,
                ).start()

            @pl.when(j == mine)
            def _():
                pltpu.make_async_copy(src.at[j], dst.at[j], self_sem.at[own]).start()

    def gathered(src, dst, send, recv, first, own):
        @pl.loop(0, near)
        def _(j):
            @pl.when(j != mine)
            def _():
                remote(
                    src.at[j], dst.at[j], send.at[first + j], recv.at[first + j], ep=base + j
                ).wait_recv()

            @pl.when(j == mine)
            def _():
                pltpu.make_async_copy(src.at[j], dst.at[j], self_sem.at[own]).wait()

    def drained(src, dst, send, recv, first):
        @pl.loop(0, near)
        def _(j):
            @pl.when(j != mine)
            def _():
                remote(
                    src.at[j], dst.at[j], send.at[first + j], recv.at[first + j], ep=base + j
                ).wait_send()

    def forward(x, k):
        return remote(x.at[c], x.at[c], fw_send.at[k], fw_recv.at[k], tp=o)

    def expert(x, part_recv, y, k):
        rows = x.shape[1] * x.shape[2]
        part_send = ps.at[:rows]
        forward(x, k).start()
        remote(x.at[c], x.at[o], fw_send.at[k], fw_recv.at[k], tp=o).wait_recv()

        @pl.loop(0, ff // tile)
        def _(t):
            cols = pl.ds(pl.multiple_of(t * tile, tile), tile)
            hidden = jnp.dot(
                x[0].reshape(rows, half), w1_v[:half, cols], preferred_element_type=F32
            ) + jnp.dot(
                x[1].reshape(rows, half), w1_v[half:, cols], preferred_element_type=F32
            )
            h_v[:rows, cols] = jnp.maximum(hidden, 0.0).astype(BF16)

        def second(dst, side):
            @pl.loop(0, half // tile)
            def _(t):
                cols = pl.ds(pl.multiple_of(t * tile, tile), tile)
                dst[:, cols] = jnp.dot(
                    h_v[:rows], w2_v[:, pl.ds(pl.multiple_of(side * half + t * tile, tile), tile)],
                    preferred_element_type=F32,
                )

        second(part_send, o)
        part = remote(part_send, part_recv, pt_send.at[k], pt_recv.at[k], tp=o)
        part.start()
        second(yo.at[:rows], c)
        part.wait()
        y[...] = (yo[:rows] + part_recv[...]).astype(BF16).reshape(y.shape)

    def weighted(matches, gate0, gate1, values):
        weight = jnp.where(matches[0], gate0, 0.0) + jnp.where(matches[1], gate1, 0.0)
        high = weight.astype(BF16)
        low = (weight - high.astype(F32)).astype(BF16)
        dims = (((0,), (0,)), ((), ()))
        return lax.dot_general(
            high, values, dims, preferred_element_type=F32
        ) + lax.dot_general(low, values, dims, preferred_element_type=F32)

    def to_partner(s):
        return remote(nrm.at[s], pnrm.at[s], tk_send.at[s], tk_recv.at[s], ep=partner)

    def far_rows(s):
        to_partner(s).wait_recv()
        fsend[s] = picked(far_matches(s), pnrm[s], (near, caps, half))
        spread(fsend.at[s], frecv.at[s, c], ff_send, ff_recv, s * near, 2 + s)

    def far_expert(s):
        gathered(fsend.at[s], frecv.at[s, c], ff_send, ff_recv, s * near, 2 + s)
        expert(frecv.at[s], fpr.at[s], fysend.at[s], 1 + s)
        spread(fysend.at[s], fyrecv.at[s], fy_send, fy_recv, s * near, 4 + s)

    def back(s):
        return remote(cback.at[s], cmix.at[s], cb_send.at[s], cb_recv.at[s], ep=partner)

    def far_back(s):
        gathered(fysend.at[s], fyrecv.at[s], fy_send, fy_recv, s * near, 4 + s)
        cback[s] = weighted(
            far_matches(s), pmeta[s, 2:3, :], pmeta[s, 3:4, :],
            fyrecv[s].reshape(near * caps, half),
        ).astype(BF16)
        back(s).start()

    give_meta = remote(meta, pmeta, tk_send.at[2], tk_recv.at[2], ep=partner)
    give_meta.start()
    to_partner(0).start()
    xsend[...] = picked(near_matches(), nrm[...].reshape(2 * tok, half), (near, cap2, half))
    spread(xsend, xrecv.at[c], xs_send, xs_recv, 0, 0)
    to_partner(0).wait_send()
    to_partner(1).start()
    give_meta.wait_recv()
    far_rows(0)
    load_w1.wait()
    load_w2.wait()
    gathered(xsend, xrecv.at[c], xs_send, xs_recv, 0, 0)
    expert(xrecv, pr, ysend, 0)
    spread(ysend, yrecv, ys_send, ys_recv, 0, 1)
    far_expert(0)
    far_rows(1)
    far_back(0)
    far_expert(1)
    gathered(ysend, yrecv, ys_send, ys_recv, 0, 1)
    mixed[...] = weighted(
        near_matches(), lanes(2), lanes(3), yrecv[...].reshape(near * cap2, half)
    ).reshape(2, tok, half)
    far_back(1)
    for s in range(2):
        back(s).wait_recv()
        mixed[s] += cmix[s].astype(F32)

    send_m = remote(mixed.at[o], mrecv, pair_send.at[3], pair_recv.at[3], tp=o)
    send_m.start()
    own = pl.ds(pl.multiple_of(c * half, half), half)
    other = pl.ds(pl.multiple_of(o * half, half), half)
    out[:, own] = (stream_v[:, own].astype(F32) + mixed[c]).astype(BF16)
    send_m.wait_recv()
    out[:, other] = (stream_v[:, other].astype(F32) + mrecv[...]).astype(BF16)

    for send in send_p + send_n:
        send.wait_send()
    send_meta.wait_send()
    send_m.wait_send()

    give_meta.wait_send()
    to_partner(1).wait_send()
    drained(xsend, xrecv.at[c], xs_send, xs_recv, 0)
    drained(ysend, yrecv, ys_send, ys_recv, 0)
    forward(xrecv, 0).wait_send()
    for s in range(2):
        drained(fsend.at[s], frecv.at[s, c], ff_send, ff_recv, s * near)
        drained(fysend.at[s], fyrecv.at[s], fy_send, fy_recv, s * near)
        forward(frecv.at[s], 1 + s).wait_send()
        back(s).wait_send()


def body(
    n,
    context,
    out_weight,
    residual_in,
    norm_gain,
    expert_ids,
    gate_weights,
    keep_mask,
    expert_in,
    expert_out,
):
    tok, width = residual_in.shape[1:]
    heads = out_weight.shape[0]
    ff = expert_in.shape[2]
    half = width // 2
    cap = 3 * tok // n
    cap2 = -(-2 * cap // 16) * 16
    caps = -(-cap // 16) * 16
    near = n // 2
    wide, narrow = near * cap2, near * caps
    vmem = pl.BlockSpec(memory_space=pltpu.VMEM)
    hbm = pl.BlockSpec(memory_space=pl.ANY)
    dma = pltpu.SemaphoreType.DMA
    result = pl.pallas_call(
        functools.partial(kernel, n, cap, cap2, caps),
        out_shape=jax.ShapeDtypeStruct((tok, width), BF16),
        in_specs=[vmem] * 6 + [hbm, hbm, hbm],
        out_specs=vmem,
        scratch_shapes=[
            pltpu.VMEM((heads, width), BF16),
            pltpu.VMEM((width, ff), BF16),
            pltpu.VMEM((ff, width), BF16),
            pltpu.VMEM((2, tok, width), F32),
            pltpu.VMEM((tok, width), F32),
            pltpu.VMEM((tok, width), BF16),
            pltpu.VMEM((2, tok, half), BF16),
            pltpu.VMEM((2, tok, half), BF16),
            pltpu.VMEM((2, 8, tok), F32),
            pltpu.VMEM((2, tok, half), BF16),
            pltpu.VMEM((2, 8, tok), F32),
            pltpu.VMEM((near, cap2, half), BF16),
            pltpu.VMEM((2, near, cap2, half), BF16),
            pltpu.VMEM((2, near, caps, half), BF16),
            pltpu.VMEM((2, 2, near, caps, half), BF16),
            pltpu.VMEM((max(wide, narrow), ff), BF16),
            pltpu.VMEM((max(wide, narrow), half), F32),
            pltpu.VMEM((max(wide, narrow), half), F32),
            pltpu.VMEM((wide, half), F32),
            pltpu.VMEM((2, narrow, half), F32),
            pltpu.VMEM((near, cap2, half), BF16),
            pltpu.VMEM((near, cap2, half), BF16),
            pltpu.VMEM((2, near, caps, half), BF16),
            pltpu.VMEM((2, near, caps, half), BF16),
            pltpu.VMEM((2, tok, half), BF16),
            pltpu.VMEM((2, tok, half), BF16),
            pltpu.VMEM((2, tok, half), F32),
            pltpu.VMEM((tok, half), F32),
            dma((6,)), dma((8,)), dma((8,)), dma((3,)), dma((3,)),
            dma((3,)), dma((3,)), dma((3,)), dma((3,)),
            dma((near,)), dma((near,)), dma((near,)), dma((near,)),
            dma((n,)), dma((n,)), dma((n,)), dma((n,)),
            dma((2,)), dma((2,)), dma((6,)),
        ],
        compiler_params=pltpu.CompilerParams(
            collective_id=0, has_side_effects=True, vmem_limit_bytes=60 * 2**20
        ),
    )(
        context[0], residual_in[0], norm_gain[None, :],
        expert_ids[0].T, gate_weights[0].T, keep_mask[0].T,
        out_weight, expert_in[0], expert_out[0],
    )
    return result[None]


def solution(mesh):
    return jax.shard_map(
        functools.partial(body, mesh.shape["ep"]),
        mesh=mesh,
        in_specs=(
            P("ep", None, "tp"),
            P("tp", None),
            P("ep", "tp", None),
            P(),
            P("ep", "tp", None),
            P("ep", "tp", None),
            P("ep", "tp", None),
            P("ep", None, "tp"),
            P("ep", "tp", None),
        ),
        out_specs=P("ep", "tp", None),
        check_vma=False,
    )
```
